32 devices in a mesh: cluster: 8 (over y, x, core), batch: 4 (over z).
Axes of the slice: x: 2, y: 2, z: 4, core: 2. Of those that a mesh axis runs over, the one named last changes fastest.
Arguments:
- features: bfloat16 [4, 8192, 128], P('batch', 'cluster'), may hold values from -6 to 6
- tiles: bfloat16 [4, 64, 5, 128, 128], P('batch', 'cluster'), may hold values from 0 to 1
- columns: int32 [4, 64, 5], P('batch', 'cluster'), may hold values from 0 to 63, as said below
- live_blocks: int32 [4, 64], P('batch', 'cluster'), may hold values from 1 to 5, as said below
- edge_counts: int32 [4, 64, 5, 128], P('batch', 'cluster'), may hold values from 1 to 8
- weight: bfloat16 [256, 128], replicated, may hold values from -0.375 to 0.375
- bias: float32 [128], replicated, may hold values from -3 to 3
- cotangent: bfloat16 [4, 8192, 128], P('batch', 'cluster'), may hold values from -6 to 6
Outputs:
- output: bfloat16 [4, 8192, 128], P('batch', 'cluster')
- grad_features: float32 [4, 8192, 128], P('batch', 'cluster')
- grad_weight: float32 [256, 128], replicated
- grad_bias: float32 [128], replicated
The draws below stay inside these ranges and needn't reach their ends.
Inputs may be any that keep to these rules, and one draw needn't show every extreme that they name: columns[c, p, s] lies within 2 panels of p. Inside a cluster the slots of a row panel that fall inside the cluster name distinct panels; slots that would fall outside the cluster name p itself. The first live_blocks[c, p] slots of row panel p are its nonzero blocks; the others are padding.
All inputs are finite; a program needn't handle non-finite values.
Results may differ from the reference program's by a relative error of at most 0.006.
Values may be sent and summed in bfloat16 or wider, within the bound.
No kernel may reach another device: no remote copies, remote signals or barrier semaphores. Data moves between devices by JAX's collectives and lax.ppermute only.
A program may use at most 64 MiB of HBM per device.

```python
import math
from functools import partial
import jax
import jax.numpy as jnp
from jax import lax

F = 128
H = 128
BLK = 128
REACH = 2
SLOTS = 5
CLUSTERS = 4
PANELS = 64
NODES = 8192


def draw_columns(key, part):
    key = jax.random.fold_in(key, 11)
    shape = (CLUSTERS, PANELS, SLOTS)
    scores = jax.random.randint(key, shape, 0, 1 << 20)
    distinct = scores * SLOTS + lax.broadcasted_iota(jnp.int32, shape, 2)
    order = jnp.argsort(distinct, axis=2).astype(jnp.int32)
    row_panel = lax.broadcasted_iota(jnp.int32, shape, 1)
    target = row_panel + order - REACH
    inside = (target >= 0) & (target < PANELS)
    return jnp.where(inside, target, row_panel).astype(jnp.int32)


def draw_live_blocks(key, part):
    key = jax.random.fold_in(key, 23)
    shape = (CLUSTERS, PANELS)
    raw = jax.random.randint(key, shape, 0, SLOTS)
    counts = 1 + raw * raw // (SLOTS - 1)
    leading = lax.broadcasted_iota(jnp.int32, shape, 1) == 0
    return jnp.where(leading, SLOTS, counts).astype(jnp.int32)


def with_ends(values, rng, low, high):
    longest = values.shape.index(max(values.shape))
    spots = []
    for shift in (0, 1):
        where = [jax.random.randint(jax.random.fold_in(rng, axis), (), 0, length) for axis, length in enumerate(values.shape)]
        where[longest] = (where[longest] + shift) % values.shape[longest]
        spots.append(tuple(where))
    return values.at[spots[0]].set(low).at[spots[1]].set(high)


def levels(own_key, dims, pieces, low, top_value):
    def one(position, blocks):
        heights = jax.random.uniform(jax.random.fold_in(jax.random.fold_in(own_key, 6), position), (blocks,), jnp.float32, low / len(pieces), top_value / len(pieces))
        return jnp.repeat(jnp.exp(heights), dims[position] // blocks).reshape((-1,) + (1,) * (len(dims) - position - 1))

    loudness = one(*pieces[0])
    for cut in pieces[1:]:
        loudness = loudness * one(*cut)
    return loudness


def gaussian(own_key, dims, deviation, most, cuts=(), dtype=jnp.bfloat16):
    factor_of = levels(own_key, dims, cuts, -0.22, 0.18) if cuts else 1.0
    entries = jax.random.normal(own_key, dims, jnp.float32) * deviation * factor_of
    return jnp.minimum(jnp.maximum(entries, -most), most).astype(dtype)


def setup_inputs(seed: int = 0) -> dict:
    keys = jax.random.split(jax.random.key(seed), 9)
    features = gaussian(keys[0], (CLUSTERS, NODES, F), 1.0, 6.0, ((0, 4), (1, 8)))
    tiles = jnp.clip(1.0 * jax.random.uniform(keys[1], (CLUSTERS, PANELS, SLOTS, BLK, BLK), jnp.float32) ** levels(keys[1], (CLUSTERS, PANELS, SLOTS, BLK, BLK), ((0, 4), (1, 8)), -0.2, 0.2), 0.0, 1.0).astype(jnp.bfloat16)
    columns = draw_columns(jax.random.fold_in(keys[8], 71), 0)
    live_blocks = draw_live_blocks(jax.random.fold_in(keys[8], 71), 0)
    edge_counts = with_ends(jax.random.randint(keys[4], (CLUSTERS, PANELS, SLOTS, BLK), 1, 9), jax.random.fold_in(keys[4], 1), 1, 8).astype(jnp.int32)
    weight = gaussian(keys[5], (2 * F, H), (2 * F) ** -0.5, 0.375)
    bias = gaussian(keys[6], (H,), 0.5, 3.0, (), jnp.float32)
    cotangent = gaussian(keys[7], (CLUSTERS, NODES, H), 1.0, 6.0, ((0, 4), (1, 8)))
    return dict(features=features, tiles=tiles, columns=columns, live_blocks=live_blocks, edge_counts=edge_counts, weight=weight, bias=bias, cotangent=cotangent)


def silu_slope(values):
    sigmoid_v = jax.nn.sigmoid(values)
    return sigmoid_v * (1.0 + values * (1.0 - sigmoid_v))

def one_cluster(weight, bias, inputs):
    node_feats, tile_set, col_ids, live_count, count_set, cot_rows = inputs
    live_mask = (lax.broadcasted_iota(jnp.int32, (PANELS, SLOTS), 1) < live_count[:, None]).astype(jnp.float32)
    degree = lax.optimization_barrier(jnp.sum(live_mask[:, :, None] * count_set.astype(jnp.float32), axis=1))
    panel_rows = node_feats.reshape(PANELS, BLK, F)

    def gather_panel(args):
        tiles_one, cols_one, mask_one = args
        picked = panel_rows[cols_one].astype(jnp.float32)
        weighted = tiles_one.astype(jnp.float32) * mask_one[:, None, None]
        return jnp.einsum('src,scf->rf', weighted, picked)
    summed = lax.map(gather_panel, (tile_set, col_ids, live_mask))
    neighbor_mean = (summed / degree[:, :, None]).astype(jnp.bfloat16).reshape(PANELS * BLK, F)
    pre_act = jnp.dot(node_feats, weight[:F], preferred_element_type=jnp.float32)
    pre_act = pre_act + jnp.dot(neighbor_mean, weight[F:], preferred_element_type=jnp.float32) + bias
    output = jax.nn.silu(pre_act).astype(jnp.bfloat16)
    slope_bf = (cot_rows.astype(jnp.float32) * silu_slope(pre_act)).astype(jnp.bfloat16)
    joined = jnp.concatenate([node_feats, neighbor_mean], axis=1)
    weight_term = jnp.dot(joined.T, slope_bf, preferred_element_type=jnp.float32)
    bias_term = lax.optimization_barrier(jnp.sum(slope_bf.astype(jnp.float32), axis=0))
    scaled = jnp.dot(slope_bf, weight[F:].T, preferred_element_type=jnp.float32)
    scaled = (scaled / degree.reshape(PANELS * BLK)[:, None]).astype(jnp.bfloat16)
    scaled_panels = scaled.reshape(PANELS, BLK, F)

    def spread_panel(totals, args):
        tiles_one, cols_one, mask_one, rows_one = args
        weighted = tiles_one.astype(jnp.float32) * mask_one[:, None, None]
        contrib = jnp.einsum('src,rf->scf', weighted, rows_one.astype(jnp.float32))
        return (totals.at[cols_one].add(contrib), None)
    totals, unused = lax.scan(spread_panel, jnp.zeros((PANELS, BLK, F), jnp.float32), (tile_set, col_ids, live_mask, scaled_panels))
    grad_features = jnp.dot(slope_bf, weight[:F].T, preferred_element_type=jnp.float32)
    grad_features = grad_features + totals.reshape(PANELS * BLK, F)
    return (output, grad_features, weight_term, bias_term)

def reference(features, tiles, columns, live_blocks, edge_counts, weight, bias, cotangent):
    output, grad_features, weight_terms, bias_terms = lax.map(partial(one_cluster, weight, bias), (features, tiles, columns, live_blocks, edge_counts, cotangent))
    grad_scale = 1.0 / math.sqrt(CLUSTERS * NODES)
    grad_weight = lax.optimization_barrier(jnp.sum(weight_terms, axis=0)) * grad_scale
    grad_bias = lax.optimization_barrier(jnp.sum(bias_terms, axis=0)) * grad_scale
    return (output, grad_features, grad_weight, grad_bias)
```

```python
import functools
import math

import jax
import jax.numpy as jnp
from jax import lax
from jax.experimental import pallas as pl
from jax.experimental.pallas import tpu as pltpu
from jax.sharding import PartitionSpec as P

REACH = 2
TAIL = 16
F32 = jnp.float32
BF16 = jnp.bfloat16
VMEM = pl.BlockSpec(memory_space=pltpu.VMEM)
SMEM = pl.BlockSpec(memory_space=pltpu.SMEM)


def dot(a, b):
    return jnp.dot(a, b, preferred_element_type=F32)


def place():
    return lax.axis_index("cluster"), lax.axis_index("batch")


def half_of(clusters, batches):
    c, b = place()
    total = jnp.int32(0)
    for index, size in ((c, clusters), (b, batches)):
        for bit in range((size - 1).bit_length()):
            total = total + ((index >> bit) & 1)
    return total % 2


def activation(pre):
    sig = 1.0 / (1.0 + jnp.exp(-pre))
    return pre * sig, sig * (1.0 + pre * (1.0 - sig))


def split3(value):
    first = value.astype(BF16)
    rest = value - first.astype(F32)
    second = rest.astype(BF16)
    third = (rest - second.astype(F32)).astype(BF16)
    return first, second, third


def tail_rows(total):
    first, second, third = split3(jnp.broadcast_to(total, (TAIL, total.shape[1])))
    row = lax.broadcasted_iota(jnp.int32, first.shape, 0)
    zero = jnp.zeros_like(first)
    return jnp.where(row == 0, first, jnp.where(row == 1, second, jnp.where(row == 2, third, zero)))


def tail_total(rows):
    return jnp.sum(rows.astype(F32), axis=0, keepdims=True)


def edges(panels):
    par = lax.axis_index("cluster") % 2
    return (panels - REACH) * (1 - par), (panels - REACH) * par, par


def band(cols, live, tiles, base, outside, first):
    slots = tiles.shape[2]
    rows = []
    for j in range(REACH):
        p = base + j
        blocks = []
        for m in range(REACH):
            found = jnp.int32(0)
            for s in range(slots):
                hit = (s < live[0, p]) & (cols[0, p, s] - first == outside + m)
                found = found + jnp.where(hit, s + 1, 0)
            tile = tiles[0, p, jnp.maximum(found - 1, 0)]
            blocks.append(jnp.where(found > 0, tile, jnp.zeros_like(tile)))
        rows.append(jnp.concatenate(blocks, axis=1))
    return jnp.concatenate(rows, axis=0)


def own_slot(cols, live, p, s, first, panels):
    q = cols[0, p, s] - first
    return jnp.where((s < live[0, p]) & (q >= 0) & (q < panels), q, panels)


def forward_near(
    cols, live, feat, mate, tiles, counts, weight, bias, cot,
    out_near, slope_t, recip, t_far, s_far, r_far, p_far, c_far, f_far, w_part, b_part, mate_ret,
    own,
):
    panels, slots, block = tiles.shape[1], tiles.shape[2], tiles.shape[3]
    width = feat.shape[2]
    first = lax.axis_index("cluster") * panels
    edge, far, par = edges(panels)
    mid = panels - 2 * REACH
    order = [REACH + j for j in range(mid)] + [edge + j for j in range(REACH)] + [far + j for j in range(REACH)]
    near = (mid + REACH) * block
    span = REACH * block
    own[0 : panels * block, :] = feat[0]
    own[panels * block :, :] = jnp.zeros((block, width), BF16)
    rows = []
    for p in order:
        count = counts[0, p]
        slot = lax.broadcasted_iota(jnp.int32, count.shape, 0)
        kept = jnp.where(slot < live[0, p], count, 0).astype(F32)
        rows.append(jnp.sum(kept, axis=0, keepdims=True))
    recip_rows = 1.0 / jnp.concatenate(rows, axis=0)
    recip[...] = recip_rows
    recip_cols = recip_rows.T

    def own_sum(p):
        lhs = jnp.concatenate([tiles[0, p, s] for s in range(slots)], axis=1)
        rhs = []
        for s in range(slots):
            q = own_slot(cols, live, p, s, first, panels)
            rhs.append(own[pl.ds(pl.multiple_of(q * block, block), block), :])
        return dot(lhs, jnp.concatenate(rhs, axis=0))

    sums = [own_sum(p) for p in order]
    t_mate = band(cols, live, tiles, edge, panels - (panels + REACH) * par, first)
    across = dot(t_mate, mate[...])
    for j in range(REACH):
        sums[mid + j] = sums[mid + j] + across[j * block : (j + 1) * block]
    means = [(sums[j] * recip_cols[:, j : j + 1]).astype(BF16) for j in range(mid + REACH)]
    edge_rows = pl.ds(pl.multiple_of(edge * block, block), span)
    far_rows = pl.ds(pl.multiple_of(far * block, block), span)
    mid_rows = slice(REACH * block, REACH * block + mid * block)
    mean = jnp.concatenate(means, axis=0)
    node = jnp.concatenate([feat[0, mid_rows, :], feat[0, edge_rows, :]], axis=0)
    cot_near = jnp.concatenate([cot[0, mid_rows, :], cot[0, edge_rows, :]], axis=0)
    joined = jnp.concatenate([node, mean], axis=1)
    pre = dot(joined, weight[...]) + bias[...]
    act, rise = activation(pre)
    out_near[...] = act.astype(BF16)
    slope = (cot_near.astype(F32) * rise).astype(BF16)
    turned = slope.T
    slope_t[...] = turned
    w_part[...] = dot(turned, joined)
    b_part[...] = jnp.broadcast_to(jnp.sum(slope.astype(F32), axis=0, keepdims=True), b_part.shape)
    scale_row = jnp.concatenate([recip_rows[mid + j : mid + j + 1] for j in range(REACH)], axis=1)
    scaled = (dot(weight[width:, :], turned[:, mid * block :]) * scale_row).astype(BF16)
    back = dot(scaled, t_mate).astype(BF16)
    for m in range(REACH):
        mate_ret[m * block : (m + 1) * block, :] = back[:, m * block : (m + 1) * block]
    t_far[...] = band(cols, live, tiles, far, (panels + REACH) * par - REACH, first)
    for j in range(REACH):
        here = slice(j * block, (j + 1) * block)
        s_far[here, :] = sums[mid + REACH + j]
        col = recip_cols[:, mid + REACH + j : mid + REACH + j + 1]
        r_far[here, :] = jnp.broadcast_to(col, (block, width))
    f_far[...] = feat[0, far_rows, :]
    c_far[...] = cot[0, far_rows, :]
    p_far[...] = dot(feat[0, far_rows, :], weight[:width, :]) + bias[...]


def forward_far(
    halo, t_far, s_far, r_far, p_far, c_far, f_far, weight, w_part, b_part, mate_ret,
    out_far, slope_t, kept, send,
    *, clusters, batches,
):
    width = f_far.shape[1]
    half = half_of(clusters, batches)
    mean = ((s_far[...] + dot(t_far[...], halo[...])) * r_far[...]).astype(BF16)
    pre = p_far[...] + dot(mean, weight[width:, :])
    act, rise = activation(pre)
    out_far[...] = act.astype(BF16)
    slope = (c_far[...].astype(F32) * rise).astype(BF16)
    turned = slope.T
    slope_t[...] = turned
    total = w_part[...] + dot(turned, jnp.concatenate([f_far[...], mean], axis=1))
    b_total = b_part[0:1, :] + jnp.sum(slope.astype(F32), axis=0, keepdims=True)
    low, high = total[:, :width], total[:, width:]
    rows = low.shape[0]
    kept[0:rows, :] = jnp.where(half == 0, low, high)
    kept[rows:, :] = jnp.broadcast_to(b_total, (kept.shape[0] - rows, width))
    send[0:rows, :] = jnp.where(half == 0, high, low).astype(BF16)
    send[rows : rows + TAIL, :] = tail_rows(b_total)
    send[rows + TAIL :, :] = mate_ret[...]


def return_far(weight, slope_t, t_far, recip, far_ret):
    width = weight.shape[1]
    panels, block = recip.shape
    scale_row = jnp.concatenate([recip[panels - REACH + j : panels - REACH + j + 1, :] for j in range(REACH)], axis=1)
    scaled = (dot(weight[width:, :], slope_t[...]) * scale_row).astype(BF16)
    back = dot(scaled, t_far[...]).astype(BF16)
    for m in range(REACH):
        far_ret[m * block : (m + 1) * block, :] = back[:, m * block : (m + 1) * block]


def first_sum(kept, got, total):
    rows = kept.shape[0] - TAIL
    total[0:rows, :] = (kept[0:rows, :] + got[0:rows, :].astype(F32)).astype(BF16)
    total[rows:, :] = tail_rows(kept[rows : rows + 1, :] + tail_total(got[rows : rows + TAIL, :]))


def next_sum(mine, got, total):
    rows = mine.shape[0] - TAIL
    total[0:rows, :] = (mine[0:rows, :].astype(F32) + got[0:rows, :].astype(F32)).astype(total.dtype)
    b_total = tail_total(mine[rows:, :]) + tail_total(got[rows:, :])
    if total.dtype == BF16:
        total[rows:, :] = tail_rows(b_total)
    else:
        total[rows:, :] = jnp.broadcast_to(b_total, (TAIL, b_total.shape[1]))


def finish(mine, got, grad, grad_bias, *, clusters, batches, scale):
    half = half_of(clusters, batches)
    rows = got.shape[0]
    own = mine[0:rows, :].T * scale
    other = got[...].T * scale
    grad[0:rows, :] = jnp.where(half == 0, own, other)
    grad[rows:, :] = jnp.where(half == 0, other, own)
    grad_bias[...] = mine[rows : rows + 1, :] * scale


def backward(cols, live, tiles, weight, near_t, far_t, recip, total):
    panels, slots, block = tiles.shape[1], tiles.shape[2], tiles.shape[3]
    width = weight.shape[1]
    first = lax.axis_index("cluster") * panels
    edge, far, _ = edges(panels)
    mid = panels - 2 * REACH
    order = [REACH + j for j in range(mid)] + [edge + j for j in range(REACH)] + [far + j for j in range(REACH)]
    near = mid + REACH
    parts = [near_t[:, j * block : (j + 1) * block] for j in range(near)]
    parts += [far_t[:, j * block : (j + 1) * block] for j in range(REACH)]
    for j, p in enumerate(order):
        total[p] = dot(weight[:width, :], parts[j])
    total[panels] = jnp.zeros((width, block), F32)
    for j, p in enumerate(order):
        scaled = (dot(weight[width:, :], parts[j]) * recip[j : j + 1, :]).astype(BF16)
        spread = dot(scaled, jnp.concatenate([tiles[0, p, s] for s in range(slots)], axis=1))
        for s in range(slots):
            q = own_slot(cols, live, p, s, first, panels)
            total[q] = total[q] + spread[:, s * block : (s + 1) * block]


def gather_outputs(total, from_mate, from_far, out_near, out_far, grad, output):
    panels, block = total.shape[0] - 1, total.shape[2]
    edge, far, _ = edges(panels)
    mid = panels - 2 * REACH
    skip = from_mate.shape[0] - REACH * block
    for j in range(mid):
        p = REACH + j
        grad[0, p * block : (p + 1) * block, :] = total[p].T
    for base, source, start in ((edge, from_mate, skip), (far, from_far, 0)):
        for j in range(REACH):
            term = source[start + j * block : start + (j + 1) * block, :].astype(F32)
            rows = pl.ds(pl.multiple_of((base + j) * block, block), block)
            grad[0, rows, :] = (total[base + j] + term).T
    output[0, REACH * block : (REACH + mid) * block, :] = out_near[0 : mid * block, :]
    output[0, pl.ds(pl.multiple_of(edge * block, block), REACH * block), :] = out_near[mid * block :, :]
    output[0, pl.ds(pl.multiple_of(far * block, block), REACH * block), :] = out_far[...]


def call(kernel, name, shapes, specs, scratch=(), flops=0, nbytes=0, **static):
    single = not isinstance(shapes, (list, tuple))
    body = functools.partial(kernel, **static) if static else kernel
    return pl.pallas_call(
        body,
        out_shape=shapes,
        in_specs=specs,
        out_specs=VMEM if single else [VMEM] * len(shapes),
        scratch_shapes=list(scratch),
        compiler_params=pltpu.CompilerParams(vmem_limit_bytes=24 << 20),
        cost_estimate=pl.CostEstimate(flops=flops, bytes_accessed=nbytes, transcendentals=0),
        name=name,
    )


def swap(block, c_flip, b_flip):
    nc, nb = lax.axis_size("cluster"), lax.axis_size("batch")
    if b_flip == 0:
        return lax.ppermute(block, "cluster", [(c, c ^ c_flip) for c in range(nc)])
    pairs = [(c * nb + b, (c ^ c_flip) * nb + (b ^ b_flip)) for c in range(nc) for b in range(nb)]
    return lax.ppermute(block, ("cluster", "batch"), pairs)


def swap_far(block):
    n = lax.axis_size("cluster")
    return lax.ppermute(block, "cluster", [(c, (c + 1) % n if c % 2 else (c - 1) % n) for c in range(n)])


def body(features, tiles, columns, live_blocks, edge_counts, weight, bias, cotangent):
    nodes, width = features.shape[1], features.shape[2]
    panels, slots, block = tiles.shape[1], tiles.shape[2], tiles.shape[3]
    hidden = weight.shape[1]
    nc, nb = lax.axis_size("cluster"), lax.axis_size("batch")
    span = REACH * block
    near = nodes - span
    shape = jax.ShapeDtypeStruct
    par = lax.axis_index("cluster") % 2
    low, high = features[0, :span], features[0, nodes - span :]
    far_halo = swap_far(jnp.where(par == 0, low, high))
    mate_halo = swap(jnp.where(par == 0, high, low), 1, 0)
    bias_row = bias.reshape(1, hidden)
    sizes = dict(clusters=nc, batches=nb)
    (out_near, near_t, recip, t_far, s_far, r_far, p_far, c_far, f_far, w_part, b_part, mate_ret) = call(
        forward_near,
        "forward_near",
        [
            shape((near, hidden), BF16),
            shape((hidden, near), BF16),
            shape((panels, block), F32),
            shape((span, span), BF16),
            shape((span, width), F32),
            shape((span, width), F32),
            shape((span, hidden), F32),
            shape((span, hidden), BF16),
            shape((span, width), BF16),
            shape((hidden, 2 * width), F32),
            shape((8, hidden), F32),
            shape((span, block), BF16),
        ],
        [SMEM, SMEM] + [VMEM] * 7,
        [pltpu.VMEM((nodes + block, width), BF16)],
        flops=4 * 10**8,
        nbytes=4 << 20,
    )(columns, live_blocks, features, mate_halo, tiles, edge_counts, weight, bias_row, cotangent)
    rows = hidden + TAIL
    out_far, far_t, kept, send = call(
        forward_far,
        "forward_far",
        [
            shape((span, hidden), BF16),
            shape((hidden, span), BF16),
            shape((rows, width), F32),
            shape((rows + span, width), BF16),
        ],
        [VMEM] * 11,
        flops=10**8,
        nbytes=1 << 20,
        **sizes,
    )(far_halo, t_far, s_far, r_far, p_far, c_far, f_far, weight, w_part, b_part, mate_ret)
    got = swap(send, 1, 0)
    far_ret = call(return_far, "return_far", shape((span, block), BF16), [VMEM] * 4, flops=10**7, nbytes=1 << 18)(
        weight, far_t, t_far, recip
    )
    from_far = swap_far(far_ret)
    total = call(backward, "backward", shape((panels + 1, width, block), F32), [SMEM] * 2 + [VMEM] * 5, flops=4 * 10**8, nbytes=3 << 20)(
        columns, live_blocks, tiles, weight, near_t, far_t, recip
    )
    mine = call(first_sum, "first_sum", shape((rows, width), BF16), [VMEM] * 2, flops=10**5, nbytes=10**5)(kept, got)
    steps = [((1 << i) | 1, 0) for i in range(1, (nc - 1).bit_length())]
    steps += [(1, 1 << i) for i in range((nb - 1).bit_length())]
    for i, (c_flip, b_flip) in enumerate(steps):
        other = swap(mine, c_flip, b_flip)
        kind = F32 if i == len(steps) - 1 else BF16
        mine = call(next_sum, "next_sum", shape((rows, width), kind), [VMEM] * 2, flops=10**5, nbytes=10**5)(mine, other)
    last = swap(mine[:hidden], 1, 0)
    scale = 1.0 / math.sqrt(nb * nc * nodes)
    grad_weight, grad_bias = call(
        finish, "finish", [shape((2 * width, hidden), F32), shape((1, hidden), F32)], [VMEM] * 2, flops=10**5, nbytes=10**5, scale=scale, **sizes
    )(mine, last)
    grad_features, output = call(
        gather_outputs,
        "gather_outputs",
        [shape((1, nodes, width), F32), shape((1, nodes, hidden), BF16)],
        [VMEM] * 5,
        flops=10**6,
        nbytes=2 << 20,
    )(total, got, from_far, out_near, out_far)
    return output, grad_features, grad_weight, grad_bias.reshape(hidden)


def solution(mesh):
    in_specs = (
        P("batch", "cluster", None),
        P("batch", "cluster", None, None, None),
        P("batch", "cluster", None),
        P("batch", "cluster"),
        P("batch", "cluster", None, None),
        P(),
        P(),
        P("batch", "cluster", None),
    )
    out_specs = (P("batch", "cluster", None), P("batch", "cluster", None), P(), P())
    return jax.shard_map(body, mesh=mesh, in_specs=in_specs, out_specs=out_specs, check_vma=False)
```

```python
import functools
import math

import jax
import jax.numpy as jnp
from jax import lax
from jax.experimental import pallas as pl
from jax.experimental.pallas import tpu as pltpu
from jax.sharding import PartitionSpec as P

REACH = 2
TAIL = 16
F32 = jnp.float32
BF16 = jnp.bfloat16
VMEM = pl.BlockSpec(memory_space=pltpu.VMEM)
ANY = pl.BlockSpec(memory_space=pl.ANY)
HBM = pl.BlockSpec(memory_space=pltpu.HBM)
SMEM = pl.BlockSpec(memory_space=pltpu.SMEM)


def dot(a, b):
    return jnp.dot(a, b, preferred_element_type=F32)


def place():
    return lax.axis_index("cluster"), lax.axis_index("batch")


def half_of(clusters, batches):
    c, b = place()
    total = jnp.int32(0)
    for index, size in ((c, clusters), (b, batches)):
        for bit in range((size - 1).bit_length()):
            total = total + ((index >> bit) & 1)
    return total % 2


def activation(pre):
    sig = 1.0 / (1.0 + jnp.exp(-pre))
    return pre * sig, sig * (1.0 + pre * (1.0 - sig))


def split3(value):
    first = value.astype(BF16)
    rest = value - first.astype(F32)
    second = rest.astype(BF16)
    third = (rest - second.astype(F32)).astype(BF16)
    return first, second, third


def tail_rows(total):
    first, second, third = split3(jnp.broadcast_to(total, (TAIL, total.shape[1])))
    row = lax.broadcasted_iota(jnp.int32, first.shape, 0)
    zero = jnp.zeros_like(first)
    return jnp.where(row == 0, first, jnp.where(row == 1, second, jnp.where(row == 2, third, zero)))


def tail_total(rows):
    return jnp.sum(rows.astype(F32), axis=0, keepdims=True)


def edges(panels):
    par = lax.axis_index("cluster") % 2
    return (panels - REACH) * (1 - par), (panels - REACH) * par, par


def band(cols, live, tiles, base, outside, first):
    slots = tiles.shape[2]
    rows = []
    for j in range(REACH):
        p = base + j
        blocks = []
        for m in range(REACH):
            found = jnp.int32(0)
            for s in range(slots):
                hit = (s < live[0, p]) & (cols[s, 0, p] - first == outside + m)
                found = found + jnp.where(hit, s + 1, 0)
            tile = tiles[0, p, jnp.maximum(found - 1, 0)]
            blocks.append(jnp.where(found > 0, tile, jnp.zeros_like(tile)))
        rows.append(jnp.concatenate(blocks, axis=1))
    return jnp.concatenate(rows, axis=0)


def own_slot(cols, live, p, s, first, panels):
    q = cols[s, 0, p] - first
    return jnp.where((s < live[0, p]) & (q >= 0) & (q < panels), q, panels)


def pick_halo(feat, far_rows, mate_rows, sems):
    nodes, span = feat.shape[1], far_rows.shape[0]
    par = lax.axis_index("cluster") % 2
    starts = ((nodes - span) * par, (nodes - span) * (1 - par))
    copies = []
    for i, (start, rows) in enumerate(zip(starts, (far_rows, mate_rows))):
        source = feat.at[0, pl.ds(pl.multiple_of(start, span), span), :]
        copies.append(pltpu.make_async_copy(source, rows, sems.at[i]))
        copies[-1].start()
    for copy in copies:
        copy.wait()


def forward_near(
    cols, live, feat, mate, tiles, counts, weight, bias, cot,
    out_near, slope_t, recip, t_far, s_far, r_far, p_far, c_far, f_far, w_part, b_part, mate_ret,
    own,
):
    panels, slots, block = tiles.shape[1], tiles.shape[2], tiles.shape[3]
    width = feat.shape[2]
    first = lax.axis_index("cluster") * panels
    edge, far, par = edges(panels)
    mid = panels - 2 * REACH
    order = [REACH + j for j in range(mid)] + [edge + j for j in range(REACH)] + [far + j for j in range(REACH)]
    near = (mid + REACH) * block
    span = REACH * block
    own[0 : panels * block, :] = feat[0]
    own[panels * block :, :] = jnp.zeros((block, width), BF16)
    row = lax.broadcasted_iota(jnp.int32, (panels, block), 0)
    depth = jnp.zeros((panels, block), jnp.int32)
    for p in range(panels):
        depth = jnp.where(row == p, live[0, p], depth)
    degree = jnp.zeros((panels, block), jnp.int32)
    for s in range(slots):
        degree = degree + jnp.where(depth > s, counts[0, s], 0)
    inverse = 1.0 / degree.astype(F32)
    low, middle, high = inverse[:REACH], inverse[REACH : panels - REACH], inverse[panels - REACH :]
    recip_rows = jnp.where(
        par == 0,
        jnp.concatenate([middle, high, low], axis=0),
        jnp.concatenate([middle, low, high], axis=0),
    )
    recip[...] = recip_rows
    recip_cols = recip_rows.T

    def own_sum(p):
        lhs = jnp.concatenate([tiles[0, p, s] for s in range(slots)], axis=1)
        rhs = []
        for s in range(slots):
            q = own_slot(cols, live, p, s, first, panels)
            rhs.append(own[pl.ds(pl.multiple_of(q * block, block), block), :])
        return dot(lhs, jnp.concatenate(rhs, axis=0))

    sums = [own_sum(p) for p in order]
    t_mate = band(cols, live, tiles, edge, panels - (panels + REACH) * par, first)
    across = dot(t_mate, mate[...])
    for j in range(REACH):
        sums[mid + j] = sums[mid + j] + across[j * block : (j + 1) * block]
    means = [(sums[j] * recip_cols[:, j : j + 1]).astype(BF16) for j in range(mid + REACH)]
    edge_rows = pl.ds(pl.multiple_of(edge * block, block), span)
    far_rows = pl.ds(pl.multiple_of(far * block, block), span)
    mid_rows = slice(REACH * block, REACH * block + mid * block)
    mean = jnp.concatenate(means, axis=0)
    node = jnp.concatenate([feat[0, mid_rows, :], feat[0, edge_rows, :]], axis=0)
    cot_near = jnp.concatenate([cot[0, mid_rows, :], cot[0, edge_rows, :]], axis=0)
    joined = jnp.concatenate([node, mean], axis=1)
    pre = dot(joined, weight[...]) + bias[...]
    act, rise = activation(pre)
    out_near[...] = act.astype(BF16)
    slope = (cot_near.astype(F32) * rise).astype(BF16)
    turned = slope.T
    slope_t[...] = turned
    w_part[...] = dot(turned, joined)
    b_part[...] = jnp.broadcast_to(jnp.sum(slope.astype(F32), axis=0, keepdims=True), b_part.shape)
    scale_row = jnp.concatenate([recip_rows[mid + j : mid + j + 1] for j in range(REACH)], axis=1)
    scaled = (dot(weight[width:, :], turned[:, mid * block :]) * scale_row).astype(BF16)
    back = dot(scaled, t_mate).astype(BF16)
    for m in range(REACH):
        mate_ret[m * block : (m + 1) * block, :] = back[:, m * block : (m + 1) * block]
    t_far[...] = band(cols, live, tiles, far, (panels + REACH) * par - REACH, first)
    for j in range(REACH):
        here = slice(j * block, (j + 1) * block)
        s_far[here, :] = sums[mid + REACH + j]
        col = recip_cols[:, mid + REACH + j : mid + REACH + j + 1]
        r_far[here, :] = jnp.broadcast_to(col, (block, width))
    f_far[...] = feat[0, far_rows, :]
    c_far[...] = cot[0, far_rows, :]
    p_far[...] = dot(feat[0, far_rows, :], weight[:width, :]) + bias[...]


def forward_far(
    halo, t_far, s_far, r_far, p_far, c_far, f_far, weight, w_part, b_part, mate_ret,
    out_far, slope_t, kept, send,
    *, clusters, batches,
):
    width = f_far.shape[1]
    half = half_of(clusters, batches)
    mean = ((s_far[...] + dot(t_far[...], halo[...])) * r_far[...]).astype(BF16)
    pre = p_far[...] + dot(mean, weight[width:, :])
    act, rise = activation(pre)
    out_far[...] = act.astype(BF16)
    slope = (c_far[...].astype(F32) * rise).astype(BF16)
    turned = slope.T
    slope_t[...] = turned
    total = w_part[...] + dot(turned, jnp.concatenate([f_far[...], mean], axis=1))
    b_total = b_part[0:1, :] + jnp.sum(slope.astype(F32), axis=0, keepdims=True)
    low, high = total[:, :width], total[:, width:]
    rows = low.shape[0]
    kept[0:rows, :] = jnp.where(half == 0, low, high)
    kept[rows:, :] = jnp.broadcast_to(b_total, (kept.shape[0] - rows, width))
    send[0:rows, :] = jnp.where(half == 0, high, low).astype(BF16)
    send[rows : rows + TAIL, :] = tail_rows(b_total)
    send[rows + TAIL :, :] = mate_ret[...]


def return_far(weight, slope_t, t_far, recip, far_ret):
    width = weight.shape[1]
    panels, block = recip.shape
    scale_row = jnp.concatenate([recip[panels - REACH + j : panels - REACH + j + 1, :] for j in range(REACH)], axis=1)
    scaled = (dot(weight[width:, :], slope_t[...]) * scale_row).astype(BF16)
    back = dot(scaled, t_far[...]).astype(BF16)
    for m in range(REACH):
        far_ret[m * block : (m + 1) * block, :] = back[:, m * block : (m + 1) * block]


def first_sum(kept, got, far_ret, total, far_out):
    rows = kept.shape[0] - TAIL
    far_out[...] = far_ret[...]
    total[0:rows, :] = (kept[0:rows, :] + got[0:rows, :].astype(F32)).astype(BF16)
    total[rows:, :] = tail_rows(kept[rows : rows + 1, :] + tail_total(got[rows : rows + TAIL, :]))


def next_sum(mine, got, total):
    rows = mine.shape[0] - TAIL
    total[0:rows, :] = (mine[0:rows, :].astype(F32) + got[0:rows, :].astype(F32)).astype(BF16)
    total[rows:, :] = tail_rows(tail_total(mine[rows:, :]) + tail_total(got[rows:, :]))


def last_sum(mine, got, total):
    rows = mine.shape[0] - TAIL
    total[0:rows, :] = mine[0:rows, :].astype(F32) + got[0:rows, :].astype(F32)
    b_total = tail_total(mine[rows:, :]) + tail_total(got[rows:, :])
    total[rows:, :] = jnp.broadcast_to(b_total, (total.shape[0] - rows, b_total.shape[1]))


def finish(mine, got, grad, grad_bias, *, clusters, batches, scale):
    half = half_of(clusters, batches)
    rows = grad.shape[0] // 2
    own = mine[0:rows, :].T * scale
    other = got[0:rows, :].T * scale
    grad[0:rows, :] = jnp.where(half == 0, own, other)
    grad[rows:, :] = jnp.where(half == 0, other, own)
    grad_bias[...] = jnp.where(half == 0, mine[rows : rows + 1, :], got[rows : rows + 1, :]) * scale


def spread(cols, live, tiles, weight, parts, recip, total, panel_list, first_row):
    panels, slots, block = tiles.shape[1], tiles.shape[2], tiles.shape[3]
    width = weight.shape[1]
    first = lax.axis_index("cluster") * panels
    for j, p in enumerate(panel_list):
        row = recip[first_row + j : first_row + j + 1, :]
        scaled = (dot(weight[width:, :], parts[j]) * row).astype(BF16)
        terms = dot(scaled, jnp.concatenate([tiles[0, p, s] for s in range(slots)], axis=1))
        for s in range(slots):
            q = own_slot(cols, live, p, s, first, panels)
            total[q] = total[q] + terms[:, s * block : (s + 1) * block]


def backward_mid(cols, live, tiles, weight, near_t, far_t, recip, total):
    panels, block = tiles.shape[1], tiles.shape[3]
    width = weight.shape[1]
    edge, far, _ = edges(panels)
    mid = panels - 2 * REACH
    parts = [near_t[:, j * block : (j + 1) * block] for j in range(mid + REACH)]
    parts += [far_t[:, j * block : (j + 1) * block] for j in range(REACH)]
    order = [REACH + j for j in range(mid)] + [edge + j for j in range(REACH)] + [far + j for j in range(REACH)]
    for j, p in enumerate(order):
        total[p] = dot(weight[:width, :], parts[j])
    total[panels] = jnp.zeros((width, block), F32)
    spread(cols, live, tiles, weight, parts, recip, total, order[:mid], 0)


def backward_rim(cols, live, tiles, weight, near_t, far_t, recip, before, total):
    panels, block = tiles.shape[1], tiles.shape[3]
    edge, far, _ = edges(panels)
    mid = panels - 2 * REACH
    parts = [near_t[:, j * block : (j + 1) * block] for j in range(mid, mid + REACH)]
    parts += [far_t[:, j * block : (j + 1) * block] for j in range(REACH)]
    total[...] = before[...]
    order = [edge + j for j in range(REACH)] + [far + j for j in range(REACH)]
    spread(cols, live, tiles, weight, parts, recip, total, order, mid)


def gather_outputs(total, from_mate, from_far, out_near, out_far, grad, output, token):
    token[...] = jnp.zeros(token.shape, F32)
    panels, block = total.shape[0] - 1, total.shape[2]
    edge, far, _ = edges(panels)
    mid = panels - 2 * REACH
    skip = from_mate.shape[0] - REACH * block
    for j in range(mid):
        p = REACH + j
        grad[0, p * block : (p + 1) * block, :] = total[p].T
    for base, source, start in ((edge, from_mate, skip), (far, from_far, 0)):
        for j in range(REACH):
            term = source[start + j * block : start + (j + 1) * block, :].astype(F32)
            rows = pl.ds(pl.multiple_of((base + j) * block, block), block)
            grad[0, rows, :] = (total[base + j] + term).T
    output[0, REACH * block : (REACH + mid) * block, :] = out_near[0 : mid * block, :]
    output[0, pl.ds(pl.multiple_of(edge * block, block), REACH * block), :] = out_near[mid * block :, :]
    output[0, pl.ds(pl.multiple_of(far * block, block), REACH * block), :] = out_far[...]


def call(kernel, name, shapes, specs, scratch=(), micros=1.0, after=0, **static):
    single = not isinstance(shapes, (list, tuple))
    inputs = len(specs)

    def ordered(*refs):
        kernel(*refs[:inputs], *refs[inputs + after :], **static)

    return pl.pallas_call(
        ordered,
        out_shape=shapes,
        in_specs=list(specs) + [ANY] * after,
        out_specs=VMEM if single else [VMEM] * len(shapes),
        scratch_shapes=list(scratch),
        compiler_params=pltpu.CompilerParams(vmem_limit_bytes=24 << 20),
        cost_estimate=pl.CostEstimate(flops=int(micros * 10**9), bytes_accessed=1 << 16, transcendentals=0),
        name=name,
    )


def swap_chip(block):
    nc = lax.axis_size("cluster")
    return lax.ppermute(block, "cluster", [(c, c ^ 1) for c in range(nc)])


def swap_flips(block, flips):
    nc, nb = lax.axis_size("cluster"), lax.axis_size("batch")
    pairs = []
    for c in range(nc):
        for b in range(nb):
            c_flip, b_flip = flips[(c.bit_count() + b.bit_count()) % 2]
            pairs.append((c * nb + b, (c ^ c_flip ^ 1) * nb + (b ^ b_flip)))
    return lax.ppermute(block, ("cluster", "batch"), pairs)


def swap_far(block):
    nc, nb = lax.axis_size("cluster"), lax.axis_size("batch")
    pairs = []
    for c in range(nc):
        for b in range(nb):
            other = c + 1 if c % 2 else c - 1
            if 0 <= other < nc:
                pairs.append((c * nb + b, other * nb + b))
            else:
                pairs.append((c * nb + b, c * nb + (b ^ 1)))
    return lax.ppermute(block, ("cluster", "batch"), pairs)


def body(features, tiles, columns, live_blocks, edge_counts, weight, bias, cotangent):
    nodes, width = features.shape[1], features.shape[2]
    panels, slots, block = tiles.shape[1], tiles.shape[2], tiles.shape[3]
    hidden = weight.shape[1]
    nc, nb = lax.axis_size("cluster"), lax.axis_size("batch")
    span = REACH * block
    near = nodes - span
    rows = hidden + TAIL
    shape = jax.ShapeDtypeStruct
    sizes = dict(clusters=nc, batches=nb)
    columns = jnp.transpose(columns, (2, 0, 1))
    edge_counts = jnp.transpose(edge_counts, (0, 2, 1, 3))
    bias_row = bias.reshape(1, hidden)
    far_rows, mate_rows = call(
        pick_halo,
        "pick_halo",
        [shape((span, width), BF16)] * 2,
        [HBM],
        [pltpu.SemaphoreType.DMA((2,))],
        micros=8.0,
    )(features)
    mate_halo = swap_chip(mate_rows)
    far_halo = swap_far(far_rows)
    (out_near, near_t, recip, t_far, s_far, r_far, p_far, c_far, f_far, w_part, b_part, mate_ret) = call(
        forward_near,
        "forward_near",
        [
            shape((near, hidden), BF16),
            shape((hidden, near), BF16),
            shape((panels, block), F32),
            shape((span, span), BF16),
            shape((span, width), F32),
            shape((span, width), F32),
            shape((span, hidden), F32),
            shape((span, hidden), BF16),
            shape((span, width), BF16),
            shape((hidden, 2 * width), F32),
            shape((8, hidden), F32),
            shape((span, block), BF16),
        ],
        [SMEM, SMEM] + [VMEM] * 7,
        [pltpu.VMEM((nodes + block, width), BF16)],
        micros=2.0,
    )(columns, live_blocks, features, mate_halo, tiles, edge_counts, weight, bias_row, cotangent)
    out_far, far_t, kept, send = call(
        forward_far,
        "forward_far",
        [
            shape((span, hidden), BF16),
            shape((hidden, span), BF16),
            shape((rows, width), F32),
            shape((rows + span, width), BF16),
        ],
        [VMEM] * 11,
        **sizes,
    )(far_halo, t_far, s_far, r_far, p_far, c_far, f_far, weight, w_part, b_part, mate_ret)
    got = swap_chip(send)
    far_ret = call(return_far, "return_far", shape((span, block), BF16), [VMEM] * 4, micros=0.3)(
        weight, far_t, t_far, recip
    )
    mine, far_ret = call(
        first_sum, "first_sum", [shape((rows, width), BF16), shape((span, block), BF16)], [VMEM] * 3, micros=0.1
    )(kept, got, far_ret)
    made = {}

    def exchange_far(mine):
        made["from_far"] = swap_far(far_ret)
        return ()

    def sum_mid(mine):
        made["total"] = call(
            backward_mid, "backward_mid", shape((panels + 1, width, block), F32), [SMEM] * 2 + [VMEM] * 5, micros=1.2, after=1
        )(columns, live_blocks, tiles, weight, near_t, far_t, recip, mine)
        return (made["total"],)

    def sum_rim(mine):
        made["total"] = call(
            backward_rim, "backward_rim", shape((panels + 1, width, block), F32), [SMEM] * 2 + [VMEM] * 6, micros=1.2, after=1
        )(columns, live_blocks, tiles, weight, near_t, far_t, recip, made["total"], mine)
        return (made["total"],)

    def write_outputs(mine):
        grad_features, output, token = call(
            gather_outputs,
            "gather_outputs",
            [shape((1, nodes, width), F32), shape((1, nodes, hidden), BF16), shape((8, hidden), F32)],
            [VMEM] * 5,
            after=1,
        )(made["total"], got, made["from_far"], out_near, out_far, mine)
        made["outputs"] = output, grad_features
        return (token,)

    tasks = [exchange_far, sum_mid, sum_rim, write_outputs]
    bits = [(1 << i, 0) for i in range(1, (nc - 1).bit_length())] + [(0, 1 << i) for i in range((nb - 1).bit_length())]
    turn = len(bits) // 2
    steps = list(zip(bits, bits[turn:] + bits[:turn]))
    for i, flips in enumerate(steps):
        other = swap_flips(mine, flips)
        held = tasks.pop(0)(mine) if tasks else ()
        if i < len(steps) - 1:
            mine = call(next_sum, "next_sum", shape((rows, width), BF16), [VMEM] * 2, micros=0.1, after=len(held))(
                mine, other, *held
            )
        else:
            mine = call(
                last_sum, "last_sum", shape((hidden + 8, width), F32), [VMEM] * 2, micros=0.1, after=len(held)
            )(mine, other, *held)
    for task in tasks:
        task(mine)
    last = swap_chip(mine)
    scale = 1.0 / math.sqrt(nb * nc * nodes)
    grad_weight, grad_bias = call(
        finish, "finish", [shape((2 * width, hidden), F32), shape((1, hidden), F32)], [VMEM] * 2, scale=scale, **sizes
    )(mine, last)
    return *made["outputs"], grad_weight, grad_bias.reshape(hidden)


def solution(mesh):
    in_specs = (
        P("batch", "cluster", None),
        P("batch", "cluster", None, None, None),
        P("batch", "cluster", None),
        P("batch", "cluster"),
        P("batch", "cluster", None, None),
        P(),
        P(),
        P("batch", "cluster", None),
    )
    out_specs = (P("batch", "cluster", None), P("batch", "cluster", None), P(), P())
    return jax.shard_map(body, mesh=mesh, in_specs=in_specs, out_specs=out_specs, check_vma=False)
```

```python
import functools
import math

import jax
import jax.numpy as jnp
from jax import lax
from jax.experimental import pallas as pl
from jax.experimental.pallas import tpu as pltpu
from jax.sharding import PartitionSpec as P

REACH = 2
TAIL = 16
F32 = jnp.float32
BF16 = jnp.bfloat16
VMEM = pl.BlockSpec(memory_space=pltpu.VMEM)
ANY = pl.BlockSpec(memory_space=pl.ANY)
SMEM = pl.BlockSpec(memory_space=pltpu.SMEM)


def dot(a, b):
    return jnp.dot(a, b, preferred_element_type=F32)


def place():
    return lax.axis_index("cluster"), lax.axis_index("batch")


def half_of(clusters, batches):
    c, b = place()
    total = jnp.int32(0)
    for index, size in ((c, clusters), (b, batches)):
        for bit in range((size - 1).bit_length()):
            total = total + ((index >> bit) & 1)
    return total % 2


def activation(pre):
    sig = 1.0 / (1.0 + jnp.exp(-pre))
    return pre * sig, sig * (1.0 + pre * (1.0 - sig))


def split3(value):
    first = value.astype(BF16)
    rest = value - first.astype(F32)
    second = rest.astype(BF16)
    third = (rest - second.astype(F32)).astype(BF16)
    return first, second, third


def tail_rows(total):
    first, second, third = split3(jnp.broadcast_to(total, (TAIL, total.shape[1])))
    row = lax.broadcasted_iota(jnp.int32, first.shape, 0)
    zero = jnp.zeros_like(first)
    return jnp.where(row == 0, first, jnp.where(row == 1, second, jnp.where(row == 2, third, zero)))


def tail_total(rows):
    return jnp.sum(rows.astype(F32), axis=0, keepdims=True)


def edges(panels):
    par = lax.axis_index("cluster") % 2
    return (panels - REACH) * (1 - par), (panels - REACH) * par, par


def band(cols, live, tiles, base, outside, first):
    slots = tiles.shape[2]
    rows = []
    for j in range(REACH):
        p = base + j
        blocks = []
        for m in range(REACH):
            found = jnp.int32(0)
            for s in range(slots):
                hit = (s < live[0, p]) & (cols[s, 0, p] - first == outside + m)
                found = found + jnp.where(hit, s + 1, 0)
            tile = tiles[0, p, jnp.maximum(found - 1, 0)]
            blocks.append(jnp.where(found > 0, tile, jnp.zeros_like(tile)))
        rows.append(jnp.concatenate(blocks, axis=1))
    return jnp.concatenate(rows, axis=0)


def own_slot(cols, live, p, s, first, panels):
    q = cols[s, 0, p] - first
    return jnp.where((s < live[0, p]) & (q >= 0) & (q < panels), q, panels)


def pick_halo(low, high, far_rows, mate_rows):
    par = lax.axis_index("cluster") % 2
    far_rows[...] = jnp.where(par == 0, low[...], high[...])
    mate_rows[...] = jnp.where(par == 0, high[...], low[...])


def forward_near(
    cols, live, feat, mate, tiles, counts, weight, bias, cot,
    out_near, slope_t, recip, t_far, s_far, r_far, p_far, c_far, f_far, w_part, b_part, mate_ret,
    own,
):
    panels, slots, block = tiles.shape[1], tiles.shape[2], tiles.shape[3]
    width = feat.shape[2]
    first = lax.axis_index("cluster") * panels
    edge, far, par = edges(panels)
    mid = panels - 2 * REACH
    order = [REACH + j for j in range(mid)] + [edge + j for j in range(REACH)] + [far + j for j in range(REACH)]
    near = (mid + REACH) * block
    span = REACH * block
    own[0 : panels * block, :] = feat[0]
    own[panels * block :, :] = jnp.zeros((block, width), BF16)
    row = lax.broadcasted_iota(jnp.int32, (panels, block), 0)
    depth = jnp.zeros((panels, block), jnp.int32)
    for p in range(panels):
        depth = jnp.where(row == p, live[0, p], depth)
    degree = jnp.zeros((panels, block), jnp.int32)
    for s in range(slots):
        degree = degree + jnp.where(depth > s, counts[0, s], 0)
    inverse = 1.0 / degree.astype(F32)
    low, middle, high = inverse[:REACH], inverse[REACH : panels - REACH], inverse[panels - REACH :]
    recip_rows = jnp.where(
        par == 0,
        jnp.concatenate([middle, high, low], axis=0),
        jnp.concatenate([middle, low, high], axis=0),
    )
    recip[...] = recip_rows
    recip_cols = recip_rows.T

    def own_sum(p):
        lhs = jnp.concatenate([tiles[0, p, s] for s in range(slots)], axis=1)
        rhs = []
        for s in range(slots):
            q = own_slot(cols, live, p, s, first, panels)
            rhs.append(own[pl.ds(pl.multiple_of(q * block, block), block), :])
        return dot(lhs, jnp.concatenate(rhs, axis=0))

    sums = [own_sum(p) for p in order]
    t_mate = band(cols, live, tiles, edge, panels - (panels + REACH) * par, first)
    across = dot(t_mate, mate[...])
    for j in range(REACH):
        sums[mid + j] = sums[mid + j] + across[j * block : (j + 1) * block]
    means = [(sums[j] * recip_cols[:, j : j + 1]).astype(BF16) for j in range(mid + REACH)]
    edge_rows = pl.ds(pl.multiple_of(edge * block, block), span)
    far_rows = pl.ds(pl.multiple_of(far * block, block), span)
    mid_rows = slice(REACH * block, REACH * block + mid * block)
    mean = jnp.concatenate(means, axis=0)
    node = jnp.concatenate([feat[0, mid_rows, :], feat[0, edge_rows, :]], axis=0)
    cot_near = jnp.concatenate([cot[0, mid_rows, :], cot[0, edge_rows, :]], axis=0)
    joined = jnp.concatenate([node, mean], axis=1)
    pre = dot(joined, weight[...]) + bias[...]
    act, rise = activation(pre)
    out_near[...] = act.astype(BF16)
    slope = (cot_near.astype(F32) * rise).astype(BF16)
    turned = slope.T
    slope_t[...] = turned
    w_part[...] = dot(turned, joined)
    b_part[...] = jnp.broadcast_to(jnp.sum(slope.astype(F32), axis=0, keepdims=True), b_part.shape)
    scale_row = jnp.concatenate([recip_rows[mid + j : mid + j + 1] for j in range(REACH)], axis=1)
    scaled = (dot(weight[width:, :], turned[:, mid * block :]) * scale_row).astype(BF16)
    back = dot(scaled, t_mate).astype(BF16)
    for m in range(REACH):
        mate_ret[m * block : (m + 1) * block, :] = back[:, m * block : (m + 1) * block]
    t_far[...] = band(cols, live, tiles, far, (panels + REACH) * par - REACH, first)
    for j in range(REACH):
        here = slice(j * block, (j + 1) * block)
        s_far[here, :] = sums[mid + REACH + j]
        col = recip_cols[:, mid + REACH + j : mid + REACH + j + 1]
        r_far[here, :] = jnp.broadcast_to(col, (block, width))
    f_far[...] = feat[0, far_rows, :]
    c_far[...] = cot[0, far_rows, :]
    p_far[...] = dot(feat[0, far_rows, :], weight[:width, :]) + bias[...]


def forward_far(
    halo, t_far, s_far, r_far, p_far, c_far, f_far, weight, w_part, b_part, mate_ret,
    out_far, slope_t, kept, send,
    *, clusters, batches,
):
    width = f_far.shape[1]
    half = half_of(clusters, batches)
    mean = ((s_far[...] + dot(t_far[...], halo[...])) * r_far[...]).astype(BF16)
    pre = p_far[...] + dot(mean, weight[width:, :])
    act, rise = activation(pre)
    out_far[...] = act.astype(BF16)
    slope = (c_far[...].astype(F32) * rise).astype(BF16)
    turned = slope.T
    slope_t[...] = turned
    total = w_part[...] + dot(turned, jnp.concatenate([f_far[...], mean], axis=1))
    b_total = b_part[0:1, :] + jnp.sum(slope.astype(F32), axis=0, keepdims=True)
    low, high = total[:, :width], total[:, width:]
    rows = low.shape[0]
    kept[0:rows, :] = jnp.where(half == 0, low, high)
    kept[rows:, :] = jnp.broadcast_to(b_total, (kept.shape[0] - rows, width))
    send[0:rows, :] = jnp.where(half == 0, high, low).astype(BF16)
    send[rows : rows + TAIL, :] = tail_rows(b_total)
    send[rows + TAIL :, :] = mate_ret[...]


def return_far(weight, slope_t, t_far, recip, far_ret):
    width = weight.shape[1]
    panels, block = recip.shape
    scale_row = jnp.concatenate([recip[panels - REACH + j : panels - REACH + j + 1, :] for j in range(REACH)], axis=1)
    scaled = (dot(weight[width:, :], slope_t[...]) * scale_row).astype(BF16)
    back = dot(scaled, t_far[...]).astype(BF16)
    for m in range(REACH):
        far_ret[m * block : (m + 1) * block, :] = back[:, m * block : (m + 1) * block]


def first_sum(kept, got, far_ret, total, far_out):
    rows = kept.shape[0] - TAIL
    far_out[...] = far_ret[...]
    total[0:rows, :] = (kept[0:rows, :] + got[0:rows, :].astype(F32)).astype(BF16)
    total[rows:, :] = tail_rows(kept[rows : rows + 1, :] + tail_total(got[rows : rows + TAIL, :]))


def next_sum(mine, got, total):
    rows = mine.shape[0] - TAIL
    total[0:rows, :] = (mine[0:rows, :].astype(F32) + got[0:rows, :].astype(F32)).astype(BF16)
    total[rows:, :] = tail_rows(tail_total(mine[rows:, :]) + tail_total(got[rows:, :]))


def last_sum(mine, got, total):
    rows = mine.shape[0] - TAIL
    total[0:rows, :] = mine[0:rows, :].astype(F32) + got[0:rows, :].astype(F32)
    b_total = tail_total(mine[rows:, :]) + tail_total(got[rows:, :])
    total[rows:, :] = jnp.broadcast_to(b_total, (total.shape[0] - rows, b_total.shape[1]))


def finish(mine, got, grad, grad_bias, *, clusters, batches, scale):
    half = half_of(clusters, batches)
    rows = grad.shape[0] // 2
    own = mine[0:rows, :].T * scale
    other = got[0:rows, :].T * scale
    grad[0:rows, :] = jnp.where(half == 0, own, other)
    grad[rows:, :] = jnp.where(half == 0, other, own)
    grad_bias[...] = jnp.where(half == 0, mine[rows : rows + 1, :], got[rows : rows + 1, :]) * scale


def spread(cols, live, tiles, weight, turned, recip, total, panel_list, first_row):
    panels, slots, block = tiles.shape[1], tiles.shape[2], tiles.shape[3]
    width = weight.shape[1]
    first = lax.axis_index("cluster") * panels
    both = dot(weight[...], turned)
    for j, p in enumerate(panel_list):
        here = slice(j * block, (j + 1) * block)
        total[p] = total[p] + both[:width, here]
        row = recip[first_row + j : first_row + j + 1, :]
        scaled = (both[width:, here] * row).astype(BF16)
        terms = dot(scaled, jnp.concatenate([tiles[0, p, s] for s in range(slots)], axis=1))
        for s in range(slots):
            q = own_slot(cols, live, p, s, first, panels)
            total[q] = total[q] + terms[:, s * block : (s + 1) * block]


def backward_mid(cols, live, tiles, weight, near_t, recip, total):
    panels, block = tiles.shape[1], tiles.shape[3]
    mid = panels - 2 * REACH
    total[...] = jnp.zeros(total.shape, F32)
    spread(cols, live, tiles, weight, near_t[:, : mid * block], recip, total, [REACH + j for j in range(mid)], 0)


def backward_rim(cols, live, tiles, weight, near_t, far_t, recip, before, total):
    panels, block = tiles.shape[1], tiles.shape[3]
    mid = panels - 2 * REACH
    edge, far, _ = edges(panels)
    total[...] = before[...]
    order = [edge + j for j in range(REACH)] + [far + j for j in range(REACH)]
    turned = jnp.concatenate([near_t[:, mid * block :], far_t[...]], axis=1)
    spread(cols, live, tiles, weight, turned, recip, total, order, panels - 2 * REACH)


def gather_outputs(total, from_mate, from_far, out_near, out_far, grad, output, token):
    token[...] = jnp.zeros(token.shape, F32)
    panels, block = total.shape[0] - 1, total.shape[2]
    edge, far, _ = edges(panels)
    mid = panels - 2 * REACH
    skip = from_mate.shape[0] - REACH * block
    for j in range(mid):
        p = REACH + j
        grad[0, p * block : (p + 1) * block, :] = total[p].T
    for base, source, start in ((edge, from_mate, skip), (far, from_far, 0)):
        for j in range(REACH):
            term = source[start + j * block : start + (j + 1) * block, :].astype(F32)
            rows = pl.ds(pl.multiple_of((base + j) * block, block), block)
            grad[0, rows, :] = (total[base + j] + term).T
    output[0, REACH * block : (REACH + mid) * block, :] = out_near[0 : mid * block, :]
    output[0, pl.ds(pl.multiple_of(edge * block, block), REACH * block), :] = out_near[mid * block :, :]
    output[0, pl.ds(pl.multiple_of(far * block, block), REACH * block), :] = out_far[...]


def call(kernel, name, shapes, specs, scratch=(), micros=1.0, after=0, **static):
    single = not isinstance(shapes, (list, tuple))
    inputs = len(specs)

    def ordered(*refs):
        kernel(*refs[:inputs], *refs[inputs + after :], **static)

    return pl.pallas_call(
        ordered,
        out_shape=shapes,
        in_specs=list(specs) + [ANY] * after,
        out_specs=VMEM if single else [VMEM] * len(shapes),
        scratch_shapes=list(scratch),
        compiler_params=pltpu.CompilerParams(vmem_limit_bytes=24 << 20),
        cost_estimate=pl.CostEstimate(flops=int(micros * 10**9), bytes_accessed=1 << 16, transcendentals=0),
        name=name,
    )


def swap_chip(block):
    nc = lax.axis_size("cluster")
    return lax.ppermute(block, "cluster", [(c, c ^ 1) for c in range(nc)])


def swap_flips(block, flips):
    nc, nb = lax.axis_size("cluster"), lax.axis_size("batch")
    pairs = []
    for c in range(nc):
        for b in range(nb):
            c_flip, b_flip = flips[(c.bit_count() + b.bit_count()) % 2]
            pairs.append((c * nb + b, (c ^ c_flip ^ 1) * nb + (b ^ b_flip)))
    return lax.ppermute(block, ("cluster", "batch"), pairs)


def swap_far(block):
    nc, nb = lax.axis_size("cluster"), lax.axis_size("batch")
    pairs = []
    for c in range(nc):
        for b in range(nb):
            other = c + 1 if c % 2 else c - 1
            if 0 <= other < nc:
                pairs.append((c * nb + b, other * nb + b))
            else:
                pairs.append((c * nb + b, c * nb + (b ^ 1)))
    return lax.ppermute(block, ("cluster", "batch"), pairs)


def body(features, tiles, columns, live_blocks, edge_counts, weight, bias, cotangent):
    nodes, width = features.shape[1], features.shape[2]
    panels, slots, block = tiles.shape[1], tiles.shape[2], tiles.shape[3]
    hidden = weight.shape[1]
    nc, nb = lax.axis_size("cluster"), lax.axis_size("batch")
    span = REACH * block
    near = nodes - span
    rows = hidden + TAIL
    shape = jax.ShapeDtypeStruct
    sizes = dict(clusters=nc, batches=nb)
    columns = jnp.transpose(columns, (2, 0, 1))
    edge_counts = jnp.transpose(edge_counts, (0, 2, 1, 3))
    bias_row = bias.reshape(1, hidden)
    far_rows, mate_rows = call(
        pick_halo,
        "pick_halo",
        [shape((span, width), BF16)] * 2,
        [VMEM] * 2,
        micros=8.0,
    )(features[0, :span], features[0, nodes - span :])
    mate_halo = swap_chip(mate_rows)
    far_halo = swap_far(far_rows)
    (out_near, near_t, recip, t_far, s_far, r_far, p_far, c_far, f_far, w_part, b_part, mate_ret) = call(
        forward_near,
        "forward_near",
        [
            shape((near, hidden), BF16),
            shape((hidden, near), BF16),
            shape((panels, block), F32),
            shape((span, span), BF16),
            shape((span, width), F32),
            shape((span, width), F32),
            shape((span, hidden), F32),
            shape((span, hidden), BF16),
            shape((span, width), BF16),
            shape((hidden, 2 * width), F32),
            shape((8, hidden), F32),
            shape((span, block), BF16),
        ],
        [SMEM, SMEM] + [VMEM] * 7,
        [pltpu.VMEM((nodes + block, width), BF16)],
        micros=2.0,
    )(columns, live_blocks, features, mate_halo, tiles, edge_counts, weight, bias_row, cotangent)
    out_far, far_t, kept, send = call(
        forward_far,
        "forward_far",
        [
            shape((span, hidden), BF16),
            shape((hidden, span), BF16),
            shape((rows, width), F32),
            shape((rows + span, width), BF16),
        ],
        [VMEM] * 11,
        **sizes,
    )(far_halo, t_far, s_far, r_far, p_far, c_far, f_far, weight, w_part, b_part, mate_ret)
    got = swap_chip(send)
    far_ret = call(return_far, "return_far", shape((span, block), BF16), [VMEM] * 4, micros=0.3)(
        weight, far_t, t_far, recip
    )
    mine, far_ret = call(
        first_sum, "first_sum", [shape((rows, width), BF16), shape((span, block), BF16)], [VMEM] * 3, micros=0.1
    )(kept, got, far_ret)
    made = {}

    def exchange_far(mine):
        made["from_far"] = swap_far(far_ret)
        return ()

    def sum_mid(mine):
        made["total"] = call(
            backward_mid, "backward_mid", shape((panels + 1, width, block), F32), [SMEM] * 2 + [VMEM] * 4, micros=1.2, after=1
        )(columns, live_blocks, tiles, weight, near_t, recip, mine)
        return (made["total"],)

    def sum_rim(mine):
        made["total"] = call(
            backward_rim, "backward_rim", shape((panels + 1, width, block), F32), [SMEM] * 2 + [VMEM] * 6, micros=1.2, after=1
        )(columns, live_blocks, tiles, weight, near_t, far_t, recip, made["total"], mine)
        return (made["total"],)

    def write_outputs(mine):
        grad_features, output, token = call(
            gather_outputs,
            "gather_outputs",
            [shape((1, nodes, width), F32), shape((1, nodes, hidden), BF16), shape((8, hidden), F32)],
            [VMEM] * 5,
            after=1,
        )(made["total"], got, made["from_far"], out_near, out_far, mine)
        made["outputs"] = output, grad_features
        return (token,)

    tasks = [exchange_far, sum_mid, sum_rim, write_outputs]
    bits = [(1 << i, 0) for i in range(1, (nc - 1).bit_length())] + [(0, 1 << i) for i in range((nb - 1).bit_length())]
    turn = len(bits) // 2
    steps = list(zip(bits, bits[turn:] + bits[:turn]))
    for i, flips in enumerate(steps):
        other = swap_flips(mine, flips)
        held = tasks.pop(0)(mine) if tasks else ()
        if i < len(steps) - 1:
            mine = call(next_sum, "next_sum", shape((rows, width), BF16), [VMEM] * 2, micros=0.1, after=len(held))(
                mine, other, *held
            )
        else:
            mine = call(
                last_sum, "last_sum", shape((hidden + 8, width), F32), [VMEM] * 2, micros=0.1, after=len(held)
            )(mine, other, *held)
    for task in tasks:
        task(mine)
    last = swap_chip(mine)
    scale = 1.0 / math.sqrt(nb * nc * nodes)
    grad_weight, grad_bias = call(
        finish, "finish", [shape((2 * width, hidden), F32), shape((1, hidden), F32)], [VMEM] * 2, scale=scale, **sizes
    )(mine, last)
    return *made["outputs"], grad_weight, grad_bias.reshape(hidden)


def solution(mesh):
    in_specs = (
        P("batch", "cluster", None),
        P("batch", "cluster", None, None, None),
        P("batch", "cluster", None),
        P("batch", "cluster"),
        P("batch", "cluster", None, None),
        P(),
        P(),
        P("batch", "cluster", None),
    )
    out_specs = (P("batch", "cluster", None), P("batch", "cluster", None), P(), P())
    return jax.shard_map(body, mesh=mesh, in_specs=in_specs, out_specs=out_specs, check_vma=False)
```

```python
import functools
import math

import jax
import jax.numpy as jnp
from jax import lax
from jax.experimental import pallas as pl
from jax.experimental.pallas import tpu as pltpu
from jax.sharding import PartitionSpec as P

REACH = 2
TAIL = 16
F32 = jnp.float32
BF16 = jnp.bfloat16
VMEM = pl.BlockSpec(memory_space=pltpu.VMEM)
ANY = pl.BlockSpec(memory_space=pl.ANY)
SMEM = pl.BlockSpec(memory_space=pltpu.SMEM)


def dot(a, b):
    return jnp.dot(a, b, preferred_element_type=F32)


def place():
    return lax.axis_index("cluster"), lax.axis_index("batch")


def half_of(clusters, batches):
    c, b = place()
    total = jnp.int32(0)
    for index, size in ((c, clusters), (b, batches)):
        for bit in range((size - 1).bit_length()):
            total = total + ((index >> bit) & 1)
    return total % 2


def activation(pre):
    sig = 1.0 / (1.0 + jnp.exp(-pre))
    return pre * sig, sig * (1.0 + pre * (1.0 - sig))


def split3(value):
    first = value.astype(BF16)
    rest = value - first.astype(F32)
    second = rest.astype(BF16)
    third = (rest - second.astype(F32)).astype(BF16)
    return first, second, third


def tail_rows(total):
    first, second, third = split3(jnp.broadcast_to(total, (TAIL, total.shape[1])))
    row = lax.broadcasted_iota(jnp.int32, first.shape, 0)
    zero = jnp.zeros_like(first)
    return jnp.where(row == 0, first, jnp.where(row == 1, second, jnp.where(row == 2, third, zero)))


def tail_total(rows):
    return jnp.sum(rows.astype(F32), axis=0, keepdims=True)


def edges(panels):
    par = lax.axis_index("cluster") % 2
    return (panels - REACH) * (1 - par), (panels - REACH) * par, par


def band(cols, live, tiles, base, outside, first):
    slots = tiles.shape[2]
    rows = []
    for j in range(REACH):
        p = base + j
        blocks = []
        for m in range(REACH):
            found = jnp.int32(0)
            for s in range(slots):
                hit = (s < live[0, p]) & (cols[s, 0, p] - first == outside + m)
                found = found + jnp.where(hit, s + 1, 0)
            tile = tiles[0, p, jnp.maximum(found - 1, 0)]
            blocks.append(jnp.where(found > 0, tile, jnp.zeros_like(tile)))
        rows.append(jnp.concatenate(blocks, axis=1))
    return jnp.concatenate(rows, axis=0)


def own_slot(cols, live, p, s, first, panels):
    q = cols[s, 0, p] - first
    return jnp.where((s < live[0, p]) & (q >= 0) & (q < panels), q, panels)


def pick_halo(low, high, far_rows, mate_rows):
    par = lax.axis_index("cluster") % 2
    far_rows[...] = jnp.where(par == 0, low[...], high[...])
    mate_rows[...] = jnp.where(par == 0, high[...], low[...])


def forward_near(
    cols, live, feat, mate, tiles, counts, weight, bias, cot,
    out_near, slope_t, recip, t_far, s_far, r_far, p_far, c_far, f_far, w_part, b_part, mate_ret,
    own,
):
    panels, slots, block = tiles.shape[1], tiles.shape[2], tiles.shape[3]
    width = feat.shape[2]
    first = lax.axis_index("cluster") * panels
    edge, far, par = edges(panels)
    mid = panels - 2 * REACH
    order = [REACH + j for j in range(mid)] + [edge + j for j in range(REACH)] + [far + j for j in range(REACH)]
    near = (mid + REACH) * block
    span = REACH * block
    own[0 : panels * block, :] = feat[0]
    own[panels * block :, :] = jnp.zeros((block, width), BF16)
    row = lax.broadcasted_iota(jnp.int32, (panels, block), 0)
    depth = jnp.zeros((panels, block), jnp.int32)
    for p in range(panels):
        depth = jnp.where(row == p, live[0, p], depth)
    degree = jnp.zeros((panels, block), jnp.int32)
    for s in range(slots):
        degree = degree + jnp.where(depth > s, counts[0, s], 0)
    inverse = 1.0 / degree.astype(F32)
    low, middle, high = inverse[:REACH], inverse[REACH : panels - REACH], inverse[panels - REACH :]
    recip_rows = jnp.where(
        par == 0,
        jnp.concatenate([middle, high, low], axis=0),
        jnp.concatenate([middle, low, high], axis=0),
    )
    recip[...] = recip_rows
    recip_cols = recip_rows.T

    def own_sum(p):
        lhs = jnp.concatenate([tiles[0, p, s] for s in range(slots)], axis=1)
        rhs = []
        for s in range(slots):
            q = own_slot(cols, live, p, s, first, panels)
            rhs.append(own[pl.ds(pl.multiple_of(q * block, block), block), :])
        return dot(lhs, jnp.concatenate(rhs, axis=0))

    sums = [own_sum(p) for p in order]
    t_mate = band(cols, live, tiles, edge, panels - (panels + REACH) * par, first)
    across = dot(t_mate, mate[...])
    for j in range(REACH):
        sums[mid + j] = sums[mid + j] + across[j * block : (j + 1) * block]
    means = [(sums[j] * recip_cols[:, j : j + 1]).astype(BF16) for j in range(mid + REACH)]
    edge_rows = pl.ds(pl.multiple_of(edge * block, block), span)
    far_rows = pl.ds(pl.multiple_of(far * block, block), span)
    mid_rows = slice(REACH * block, REACH * block + mid * block)
    mean = jnp.concatenate(means, axis=0)
    node = jnp.concatenate([feat[0, mid_rows, :], feat[0, edge_rows, :]], axis=0)
    cot_near = jnp.concatenate([cot[0, mid_rows, :], cot[0, edge_rows, :]], axis=0)
    joined = jnp.concatenate([node, mean], axis=1)
    pre = dot(joined, weight[...]) + bias[...]
    act, rise = activation(pre)
    out_near[...] = act.astype(BF16)
    slope = (cot_near.astype(F32) * rise).astype(BF16)
    turned = slope.T
    slope_t[...] = turned
    w_part[...] = dot(turned, joined).T
    b_part[...] = jnp.broadcast_to(jnp.sum(slope.astype(F32), axis=0, keepdims=True), b_part.shape)
    scale_row = jnp.concatenate([recip_rows[mid + j : mid + j + 1] for j in range(REACH)], axis=1)
    scaled = (dot(weight[width:, :], turned[:, mid * block :]) * scale_row).astype(BF16)
    back = dot(scaled, t_mate).astype(BF16)
    for m in range(REACH):
        mate_ret[m * block : (m + 1) * block, :] = back[:, m * block : (m + 1) * block]
    t_far[...] = band(cols, live, tiles, far, (panels + REACH) * par - REACH, first)
    for j in range(REACH):
        here = slice(j * block, (j + 1) * block)
        s_far[here, :] = sums[mid + REACH + j]
        col = recip_cols[:, mid + REACH + j : mid + REACH + j + 1]
        r_far[here, :] = jnp.broadcast_to(col, (block, width))
    f_far[...] = feat[0, far_rows, :]
    c_far[...] = cot[0, far_rows, :]
    p_far[...] = dot(feat[0, far_rows, :], weight[:width, :]) + bias[...]


def forward_far(
    halo, t_far, s_far, r_far, p_far, c_far, f_far, weight, w_part, b_part, mate_ret,
    out_far, slope_t, kept, send,
    *, clusters, batches,
):
    width = f_far.shape[1]
    half = half_of(clusters, batches)
    mean = ((s_far[...] + dot(t_far[...], halo[...])) * r_far[...]).astype(BF16)
    pre = p_far[...] + dot(mean, weight[width:, :])
    act, rise = activation(pre)
    out_far[...] = act.astype(BF16)
    slope = (c_far[...].astype(F32) * rise).astype(BF16)
    turned = slope.T
    slope_t[...] = turned
    total = w_part[...] + dot(jnp.concatenate([f_far[...].T, mean.T], axis=0), slope)
    b_total = b_part[0:1, :] + jnp.sum(slope.astype(F32), axis=0, keepdims=True)
    low, high = total[:width], total[width:]
    rows = low.shape[0]
    kept[0:rows, :] = jnp.where(half == 0, low, high)
    kept[rows:, :] = jnp.broadcast_to(b_total, (kept.shape[0] - rows, width))
    send[0:rows, :] = jnp.where(half == 0, high, low).astype(BF16)
    send[rows : rows + TAIL, :] = tail_rows(b_total)
    send[rows + TAIL :, :] = mate_ret[...]


def return_far(weight, slope_t, t_far, recip, far_ret):
    width = weight.shape[1]
    panels, block = recip.shape
    scale_row = jnp.concatenate([recip[panels - REACH + j : panels - REACH + j + 1, :] for j in range(REACH)], axis=1)
    scaled = (dot(weight[width:, :], slope_t[...]) * scale_row).astype(BF16)
    back = dot(scaled, t_far[...]).astype(BF16)
    for m in range(REACH):
        far_ret[m * block : (m + 1) * block, :] = back[:, m * block : (m + 1) * block]


def first_sum(kept, got, far_ret, total, far_out):
    rows = kept.shape[0] - TAIL
    far_out[...] = far_ret[...]
    total[0:rows, :] = (kept[0:rows, :] + got[0:rows, :].astype(F32)).astype(BF16)
    total[rows:, :] = tail_rows(kept[rows : rows + 1, :] + tail_total(got[rows : rows + TAIL, :]))


def next_sum(mine, got, total):
    rows = mine.shape[0] - TAIL
    total[0:rows, :] = (mine[0:rows, :].astype(F32) + got[0:rows, :].astype(F32)).astype(BF16)
    total[rows:, :] = tail_rows(tail_total(mine[rows:, :]) + tail_total(got[rows:, :]))


def last_sum(mine, got, total):
    rows = mine.shape[0] - TAIL
    total[0:rows, :] = mine[0:rows, :].astype(F32) + got[0:rows, :].astype(F32)
    b_total = tail_total(mine[rows:, :]) + tail_total(got[rows:, :])
    total[rows:, :] = jnp.broadcast_to(b_total, (total.shape[0] - rows, b_total.shape[1]))


def finish(mine, got, grad, grad_bias, *, clusters, batches, scale):
    half = half_of(clusters, batches)
    rows = grad.shape[0] // 2
    own = mine[0:rows, :].astype(F32) * scale
    other = got[0:rows, :].astype(F32) * scale
    grad[0:rows, :] = jnp.where(half == 0, own, other)
    grad[rows:, :] = jnp.where(half == 0, other, own)
    grad_bias[...] = jnp.where(half == 0, mine[rows : rows + 1, :], got[rows : rows + 1, :]) * scale


def spread(cols, live, tiles, weight, turned, recip, total, panel_list, first_row):
    panels, slots, block = tiles.shape[1], tiles.shape[2], tiles.shape[3]
    width = weight.shape[1]
    first = lax.axis_index("cluster") * panels
    both = dot(weight[...], turned)
    for j, p in enumerate(panel_list):
        here = slice(j * block, (j + 1) * block)
        total[p] = total[p] + both[:width, here]
        row = recip[first_row + j : first_row + j + 1, :]
        scaled = (both[width:, here] * row).astype(BF16)
        terms = dot(scaled, jnp.concatenate([tiles[0, p, s] for s in range(slots)], axis=1))
        for s in range(slots):
            q = own_slot(cols, live, p, s, first, panels)
            total[q] = total[q] + terms[:, s * block : (s + 1) * block]


def backward_mid(cols, live, tiles, weight, near_t, recip, total):
    panels, block = tiles.shape[1], tiles.shape[3]
    mid = panels - 2 * REACH
    total[...] = jnp.zeros(total.shape, F32)
    spread(cols, live, tiles, weight, near_t[:, : mid * block], recip, total, [REACH + j for j in range(mid)], 0)


def backward_rim(cols, live, tiles, weight, near_t, far_t, recip, before, total):
    panels, block = tiles.shape[1], tiles.shape[3]
    mid = panels - 2 * REACH
    edge, far, _ = edges(panels)
    total[...] = before[...]
    order = [edge + j for j in range(REACH)] + [far + j for j in range(REACH)]
    turned = jnp.concatenate([near_t[:, mid * block :], far_t[...]], axis=1)
    spread(cols, live, tiles, weight, turned, recip, total, order, panels - 2 * REACH)


def gather_outputs(total, from_mate, from_far, out_near, out_far, grad, output, token):
    token[...] = jnp.zeros(token.shape, F32)
    panels, block = total.shape[0] - 1, total.shape[2]
    edge, far, _ = edges(panels)
    mid = panels - 2 * REACH
    skip = from_mate.shape[0] - REACH * block
    for j in range(mid):
        p = REACH + j
        grad[0, p * block : (p + 1) * block, :] = total[p].T
    for base, source, start in ((edge, from_mate, skip), (far, from_far, 0)):
        for j in range(REACH):
            term = source[start + j * block : start + (j + 1) * block, :].astype(F32)
            rows = pl.ds(pl.multiple_of((base + j) * block, block), block)
            grad[0, rows, :] = (total[base + j] + term).T
    output[0, REACH * block : (REACH + mid) * block, :] = out_near[0 : mid * block, :]
    output[0, pl.ds(pl.multiple_of(edge * block, block), REACH * block), :] = out_near[mid * block :, :]
    output[0, pl.ds(pl.multiple_of(far * block, block), REACH * block), :] = out_far[...]


def call(kernel, name, shapes, specs, scratch=(), micros=1.0, after=0, **static):
    single = not isinstance(shapes, (list, tuple))
    inputs = len(specs)

    def ordered(*refs):
        kernel(*refs[:inputs], *refs[inputs + after :], **static)

    return pl.pallas_call(
        ordered,
        out_shape=shapes,
        in_specs=list(specs) + [ANY] * after,
        out_specs=VMEM if single else [VMEM] * len(shapes),
        scratch_shapes=list(scratch),
        compiler_params=pltpu.CompilerParams(vmem_limit_bytes=24 << 20),
        cost_estimate=pl.CostEstimate(flops=int(micros * 10**9), bytes_accessed=1 << 16, transcendentals=0),
        name=name,
    )


def swap_chip(block):
    nc = lax.axis_size("cluster")
    return lax.ppermute(block, "cluster", [(c, c ^ 1) for c in range(nc)])


def swap_flips(block, flips):
    nc, nb = lax.axis_size("cluster"), lax.axis_size("batch")
    pairs = []
    for c in range(nc):
        for b in range(nb):
            c_flip, b_flip = flips[(c.bit_count() + b.bit_count()) % 2]
            pairs.append((c * nb + b, (c ^ c_flip ^ 1) * nb + (b ^ b_flip)))
    return lax.ppermute(block, ("cluster", "batch"), pairs)


def swap_far(block):
    nc, nb = lax.axis_size("cluster"), lax.axis_size("batch")
    pairs = []
    for c in range(nc):
        for b in range(nb):
            other = c + 1 if c % 2 else c - 1
            if 0 <= other < nc:
                pairs.append((c * nb + b, other * nb + b))
            else:
                pairs.append((c * nb + b, c * nb + (b ^ 1)))
    return lax.ppermute(block, ("cluster", "batch"), pairs)


def body(features, tiles, columns, live_blocks, edge_counts, weight, bias, cotangent):
    nodes, width = features.shape[1], features.shape[2]
    panels, slots, block = tiles.shape[1], tiles.shape[2], tiles.shape[3]
    hidden = weight.shape[1]
    nc, nb = lax.axis_size("cluster"), lax.axis_size("batch")
    span = REACH * block
    near = nodes - span
    rows = width + TAIL
    shape = jax.ShapeDtypeStruct
    sizes = dict(clusters=nc, batches=nb)
    columns = jnp.transpose(columns, (2, 0, 1))
    edge_counts = jnp.transpose(edge_counts, (0, 2, 1, 3))
    bias_row = bias.reshape(1, hidden)
    far_rows, mate_rows = call(
        pick_halo,
        "pick_halo",
        [shape((span, width), BF16)] * 2,
        [VMEM] * 2,
        micros=8.0,
    )(features[0, :span], features[0, nodes - span :])
    mate_halo = swap_chip(mate_rows)
    far_halo = swap_far(far_rows)
    (out_near, near_t, recip, t_far, s_far, r_far, p_far, c_far, f_far, w_part, b_part, mate_ret) = call(
        forward_near,
        "forward_near",
        [
            shape((near, hidden), BF16),
            shape((hidden, near), BF16),
            shape((panels, block), F32),
            shape((span, span), BF16),
            shape((span, width), F32),
            shape((span, width), F32),
            shape((span, hidden), F32),
            shape((span, hidden), BF16),
            shape((span, width), BF16),
            shape((2 * width, hidden), F32),
            shape((8, hidden), F32),
            shape((span, block), BF16),
        ],
        [SMEM, SMEM] + [VMEM] * 7,
        [pltpu.VMEM((nodes + block, width), BF16)],
        micros=2.0,
    )(columns, live_blocks, features, mate_halo, tiles, edge_counts, weight, bias_row, cotangent)
    out_far, far_t, kept, send = call(
        forward_far,
        "forward_far",
        [
            shape((span, hidden), BF16),
            shape((hidden, span), BF16),
            shape((rows, hidden), F32),
            shape((rows + span, hidden), BF16),
        ],
        [VMEM] * 11,
        **sizes,
    )(far_halo, t_far, s_far, r_far, p_far, c_far, f_far, weight, w_part, b_part, mate_ret)
    got = swap_chip(send)
    far_ret = call(return_far, "return_far", shape((span, block), BF16), [VMEM] * 4, micros=0.3)(
        weight, far_t, t_far, recip
    )
    mine, far_ret = call(
        first_sum, "first_sum", [shape((rows, width), BF16), shape((span, block), BF16)], [VMEM] * 3, micros=0.1
    )(kept, got, far_ret)
    made = {}

    def exchange_far(mine):
        made["from_far"] = swap_far(far_ret)
        return ()

    def sum_mid(mine):
        made["total"] = call(
            backward_mid, "backward_mid", shape((panels + 1, width, block), F32), [SMEM] * 2 + [VMEM] * 4, micros=1.2, after=1
        )(columns, live_blocks, tiles, weight, near_t, recip, mine)
        return (made["total"],)

    def sum_rim(mine):
        made["total"] = call(
            backward_rim, "backward_rim", shape((panels + 1, width, block), F32), [SMEM] * 2 + [VMEM] * 6, micros=1.2, after=1
        )(columns, live_blocks, tiles, weight, near_t, far_t, recip, made["total"], mine)
        return (made["total"],)

    def write_outputs(mine):
        grad_features, output, token = call(
            gather_outputs,
            "gather_outputs",
            [shape((1, nodes, width), F32), shape((1, nodes, hidden), BF16), shape((8, hidden), F32)],
            [VMEM] * 5,
            after=1,
        )(made["total"], got, made["from_far"], out_near, out_far, mine)
        made["outputs"] = output, grad_features
        return (token,)

    tasks = [exchange_far, sum_mid, sum_rim, write_outputs]
    bits = [(1 << i, 0) for i in range(1, (nc - 1).bit_length())] + [(0, 1 << i) for i in range((nb - 1).bit_length())]
    turn = len(bits) // 2
    steps = list(zip(bits, bits[turn:] + bits[:turn]))
    for i, flips in enumerate(steps):
        other = swap_flips(mine, flips)
        held = tasks.pop(0)(mine) if tasks else ()
        if i < len(steps) - 1:
            mine = call(next_sum, "next_sum", shape((rows, width), BF16), [VMEM] * 2, micros=0.1, after=len(held))(
                mine, other, *held
            )
        else:
            mine = call(
                last_sum, "last_sum", shape((width + 8, hidden), F32), [VMEM] * 2, micros=0.1, after=len(held)
            )(mine, other, *held)
    for task in tasks:
        task(mine)
    last = swap_chip(mine)
    scale = 1.0 / math.sqrt(nb * nc * nodes)
    grad_weight, grad_bias = call(
        finish, "finish", [shape((2 * width, hidden), F32), shape((1, hidden), F32)], [VMEM] * 2, scale=scale, **sizes
    )(mine, last)
    return *made["outputs"], grad_weight, grad_bias.reshape(hidden)


def solution(mesh):
    in_specs = (
        P("batch", "cluster", None),
        P("batch", "cluster", None, None, None),
        P("batch", "cluster", None),
        P("batch", "cluster"),
        P("batch", "cluster", None, None),
        P(),
        P(),
        P("batch", "cluster", None),
    )
    out_specs = (P("batch", "cluster", None), P("batch", "cluster", None), P(), P())
    return jax.shard_map(body, mesh=mesh, in_specs=in_specs, out_specs=out_specs, check_vma=False)
```
